32 devices in a mesh: row: 8 (over y, x, core), col: 4 (over z).
Axes of the slice: x: 2, y: 2, z: 4, core: 2. Of those that a mesh axis runs over, the one named last changes fastest.
Arguments:
- confidence: bfloat16 [512, 128, 128], P(('row', 'col')), as said below
- item_blocks: int32 [512], P(('row', 'col')), may hold values from 0 to 3
- counts: int32 [256], P(('row', 'col')), may hold values from 0 to 2, as said below
- item_factors: bfloat16 [4096, 128], P(('row', 'col')), may hold values from -0.3125 to 0.3125
Outputs:
- solution: float32 [4096, 128], P(('row', 'col'))
- residual: float32 [4096, 128], P(('row', 'col'))
The draws below stay inside these ranges and needn't reach their ends.
Inputs may be any that keep to these rules, and one draw needn't show every extreme that they name: `counts`: every device has some owner row with all 2 slots live. `confidence`: entries are non-negative; about half of them are zero.
All inputs are finite; a program needn't handle non-finite values.
Results may differ from the reference program's by a relative error of at most 0.035.
Values may be sent and summed in bfloat16 or wider, within the bound.
No kernel may reach another device: no remote copies, remote signals or barrier semaphores. Data moves between devices by JAX's collectives and lax.ppermute only.
A program may use at most 64 MiB of HBM per device.

```python
import math
import jax
import jax.numpy as jnp
from jax import lax

K = 128
BLK = 128
CAP = 2
ITERS = 2
NT = 16
TILES = 512
USERS = 4096
ITEMS = 4096
SLAB_BLOCKS = 4
N_ROW = 8
N_COL = 4
DEVICES = 32


def draw_confidence(key, part):
    key = jax.random.fold_in(key, 11)
    key_users = jax.random.fold_in(key, 1)
    key_keep = jax.random.fold_in(key, 2)
    key_vals = jax.random.fold_in(key, 3)
    user_scale = jnp.exp(jax.random.uniform(key_users, (USERS,), jnp.float32, 0.0, math.log(10.0)))
    slot_index = jnp.arange(TILES)
    device = slot_index // NT
    owner_block = slot_index % NT // CAP * N_COL + device % N_COL
    row_scale = user_scale.reshape(DEVICES, BLK)[owner_block]
    keep = jax.random.bernoulli(key_keep, 0.5, (TILES, BLK, BLK)).astype(jnp.float32)
    values = jnp.exp(jax.random.uniform(key_vals, (TILES, BLK, BLK), jnp.float32, math.log(0.25), 0.0))
    rise = 3.0 ** (0.5 * owner_block.astype(jnp.float32) / (DEVICES - 1))
    full = keep * values * row_scale[:, :, None] * rise[:, None, None]
    return full.astype(jnp.bfloat16)


def draw_counts(key, part):
    key = jax.random.fold_in(key, 5)
    key_fill = jax.random.fold_in(key, 1)
    key_full = jax.random.fold_in(key, 2)
    entries = DEVICES * N_ROW
    filled = jax.random.randint(key_fill, (entries,), 0, CAP + 1)
    forced = jax.random.randint(key_full, (DEVICES,), 0, N_ROW)
    position = jnp.arange(entries)
    chosen = position % N_ROW == forced[position // N_ROW]
    return jnp.where(chosen, CAP, filled).astype(jnp.int32)


def touch_ends(values, stream_key, least, top_value):
    place = [jax.random.randint(jax.random.fold_in(stream_key, axis), (), 0, length) for axis, length in enumerate(values.shape)]
    longest = values.shape.index(max(values.shape))
    beside = place[:longest] + [(place[longest] + 1) % values.shape[longest]] + place[longest + 1:]
    return values.at[tuple(place)].set(least).at[tuple(beside)].set(top_value)


def block_levels(stream_key, shape, cuts, low, top_value):
    loudness, own = 1.0, jax.random.fold_in(stream_key, 6)
    for dim, parts in cuts:
        heights = jnp.exp(jax.random.uniform(jax.random.fold_in(own, dim), (parts,), jnp.float32, low / len(cuts), top_value / len(cuts)))
        loudness = loudness * jnp.repeat(heights, shape[dim] // parts).reshape([-1 if axis == dim else 1 for axis in range(len(shape))])
    return loudness


def gaussian(stream_key, extent, scale, most, pieces=(), kind=jnp.bfloat16):
    level = block_levels(stream_key, extent, pieces, -0.22, 0.18) if pieces else 1.0
    values = jax.random.normal(stream_key, extent, jnp.float32) * scale * level
    return jnp.minimum(jnp.maximum(values, -most), most).astype(kind)


def setup_inputs(seed: int = 0) -> dict:
    streams_of = jax.random.split(jax.random.key(seed), 5)
    confidence = draw_confidence(jax.random.fold_in(streams_of[4], 71), 0)
    item_blocks = touch_ends(jax.random.randint(streams_of[1], (TILES,), 0, SLAB_BLOCKS), jax.random.fold_in(streams_of[1], 1), 0, SLAB_BLOCKS - 1).astype(jnp.int32)
    counts = draw_counts(jax.random.fold_in(streams_of[4], 71), 0)
    item_factors = gaussian(streams_of[3], (ITEMS, K), 0.05, 0.3125, ((0, 32),))
    return {"confidence": confidence, "item_blocks": item_blocks, "counts": counts, "item_factors": item_factors}


ridge = 2.0


def device_rows(confidence_d, blocks_d, counts_d, slab, dir_groups):
    slots = confidence_d.shape[0]
    active = (jnp.arange(slots) % CAP) < jnp.repeat(counts_d, CAP)
    weights = confidence_d * active.astype(confidence_d.dtype)[:, None, None]
    weights = weights.reshape(N_ROW, CAP, BLK, BLK).astype(jnp.float32)
    tile_items = slab[blocks_d].reshape(N_ROW, CAP, BLK, K).astype(jnp.float32)
    if dir_groups is None:
        user_rows = jnp.einsum('gcui,gcik->guk', weights, tile_items)
    else:
        scores = jnp.einsum('guk,gcik->gcui', dir_groups.astype(jnp.float32), tile_items)
        weighted = (weights * scores).astype(jnp.bfloat16)
        user_rows = jnp.einsum('gcui,gcik->guk', weighted.astype(jnp.float32), tile_items)
    return user_rows.astype(jnp.bfloat16)


def tile_sum(confidence, item_blocks, counts, item_factors, field):
    conf_grid = confidence.reshape(N_ROW, N_COL, NT, BLK, BLK)
    block_grid = item_blocks.reshape(N_ROW, N_COL, NT)
    count_grid = counts.reshape(N_ROW, N_COL, N_ROW)
    slabs = item_factors.reshape(N_ROW, SLAB_BLOCKS, BLK, K)
    if field is None:
        grid_dirs = jnp.zeros((N_ROW, N_COL, BLK, K), jnp.bfloat16)
    else:
        grid_dirs = field.astype(jnp.bfloat16).reshape(N_ROW, N_COL, BLK, K)

    def accumulate(running, slices):
        conf_r, blocks_r, counts_r, slab_r = slices
        if field is None:
            partial_value = jax.vmap(lambda cf, bl, ct: device_rows(cf, bl, ct, slab_r, None))(conf_r, blocks_r, counts_r)
        else:
            partial_value = jax.vmap(lambda cf, bl, ct, dg: device_rows(cf, bl, ct, slab_r, dg), in_axes=(0, 0, 0, 1))(conf_r, blocks_r, counts_r, grid_dirs)
        partial_value = lax.optimization_barrier(partial_value)
        return running + jnp.swapaxes(partial_value, 0, 1).astype(jnp.float32), None

    start = jnp.zeros((N_ROW, N_COL, BLK, K), jnp.float32)
    running, _ = lax.scan(accumulate, start, (conf_grid, block_grid, count_grid, slabs))
    return running.reshape(USERS, K)


def reference(confidence, item_blocks, counts, item_factors):
    rhs = tile_sum(confidence, item_blocks, counts, item_factors, None)
    solution = jnp.zeros((USERS, K), jnp.float32)
    residual = rhs
    direction = rhs
    norm_now = jnp.sum(residual * residual)
    for iteration in range(ITERS):
        image = ridge * direction + tile_sum(confidence, item_blocks, counts, item_factors, direction)
        step_size = norm_now / jnp.sum(direction * image)
        solution = solution + step_size * direction
        residual = residual - step_size * image
        if iteration + 1 < ITERS:
            norm_next = jnp.sum(residual * residual)
            direction = residual + (norm_next / norm_now) * direction
            norm_now = norm_next
    return solution, residual
```

```python
import functools

import jax
import jax.numpy as jnp
from jax import lax
from jax.experimental import pallas as pl
from jax.experimental.pallas import tpu as pltpu
from jax.sharding import PartitionSpec as P

ridge = 2.0
VMEM_LIMIT = 48 * 1024 * 1024
BB, BQ, VV, VB, VU, CROSS, STEP = range(7)


def dot(a, b, contract):
    return lax.dot_general(a, b, ((contract[:1], contract[1:]), ((), ())), preferred_element_type=jnp.float32)


def total(a):
    return jnp.sum(a, axis=(0, 1), keepdims=True)


def load_kernel(confidence, item_blocks, counts, block, *refs):
    parcels, (blocks_here, counts_here, block_here, arrived) = refs[:-4], refs[-4:]
    groups = len(parcels)
    per_owner = confidence.shape[0] // groups
    row = lax.axis_index("row")
    pairs = [
        (confidence.at[pl.ds((row ^ shift) * per_owner, per_owner)], parcel.at[pl.ds(0, per_owner)])
        for shift, parcel in enumerate(parcels)
    ]
    pairs += [(item_blocks, blocks_here), (counts, counts_here), (block, block_here)]
    copies = [pltpu.make_async_copy(source, target, arrived.at[i]) for i, (source, target) in enumerate(pairs)]
    for copy in copies:
        copy.start()
    for copy in copies:
        copy.wait()


def pick_kernel(groups, cols, item_blocks, counts, *refs):
    blocks, parcels, slab = refs[:cols], refs[-1 - groups:-1], refs[-1]
    for shift, block in zip(col_order(cols), blocks):
        slab[shift] = block[...]
    row, col = lax.axis_index("row"), lax.axis_index("col")
    per_owner = item_blocks.shape[0] // groups
    for shift, parcel in enumerate(parcels):
        owner = row ^ shift
        first = parcel.shape[0] - per_owner
        for place in range(per_owner):
            tile = slab[item_blocks[owner * per_owner + place] ^ col]
            parcel[first + place] = jnp.where(place < counts[owner], tile, jnp.zeros_like(tile))


def krylov_kernel(whole, split, b_ref, q_ref, v_ref, u_ref, stats):
    factor_width = b_ref.shape[1]

    def tiles_of(weights, items):
        x = items[...].reshape(-1, factor_width)
        w = jnp.concatenate([weights[place] for place in range(weights.shape[0])], axis=1)
        return x, w

    def tiles():
        for parcel in whole:
            half = parcel.shape[0] // 2
            yield tiles_of(parcel.at[pl.ds(0, half)], parcel.at[pl.ds(half, half)])
        for weights, items in split:
            yield tiles_of(weights, items)

    def apply(field):
        low = field.astype(jnp.bfloat16)
        image = ridge * field
        for x, w in tiles():
            scores = dot(low, x, (1, 1))
            weighted = (w.astype(jnp.float32) * scores).astype(jnp.bfloat16)
            image = image + dot(weighted, x, (1, 0))
        return image

    b = jnp.zeros(b_ref.shape, jnp.float32)
    for x, w in tiles():
        b = b + dot(w, x, (1, 0))
    q = apply(b)
    bb, bq = total(b * b), total(b * q)
    step = jnp.where(bq > 0, bb / bq, 1.0)
    v = b - step * q
    u = apply(v)
    b_ref[...] = b
    q_ref[...] = q
    v_ref[...] = v
    u_ref[...] = u
    values = {
        BB: bb, BQ: bq, VV: total(v * v), VB: total(v * b),
        VU: total(v * u), CROSS: total(v * q + b * u), STEP: step,
    }
    lane = lax.broadcasted_iota(jnp.int32, stats.shape[1:], 1)
    packed = jnp.zeros(stats.shape[1:], jnp.float32)
    for place, value in values.items():
        packed = jnp.where(lane == place, value, packed)
    stats[0] = packed


def finish_kernel(every, own, b_ref, q_ref, v_ref, u_ref, solution_ref, residual_ref):
    def field(place):
        return every[:, 0, place:place + 1]

    norm_now = jnp.sum(field(BB), axis=0, keepdims=True)
    step_0 = norm_now / jnp.sum(field(BQ), axis=0, keepdims=True)
    c1 = step_0 / field(STEP)
    rest = 1.0 - c1
    norm_next = jnp.sum(
        c1 * c1 * field(VV) + 2.0 * c1 * rest * field(VB) + rest * rest * field(BB), axis=0, keepdims=True
    )
    turn = norm_next / norm_now
    c2 = rest + turn
    bend = jnp.sum(c1 * c1 * field(VU) + c1 * c2 * field(CROSS) + c2 * c2 * field(BQ), axis=0, keepdims=True)
    step_1 = norm_next / bend
    c1 = step_0 / own[0, :, STEP:STEP + 1]
    rest = 1.0 - c1
    c2 = rest + turn
    b, v = b_ref[...], v_ref[...]
    solution_ref[...] = step_0 * b + step_1 * (c1 * v + c2 * b)
    residual_ref[...] = c1 * v + rest * b - step_1 * (c1 * u_ref[...] + c2 * q_ref[...])


def everyone(block, axes):
    size = lax.axis_size(axes)
    copies = jnp.broadcast_to(block[None], (size, *block.shape))
    return lax.all_to_all(copies, axes, split_axis=0, concat_axis=0, tiled=True).reshape(-1, *block.shape[1:])


def col_order(size):
    return [0, *range(size - 1, 0, -1)]


def diagonals(size):
    return [shift for shift in range(size) if (shift >> 1).bit_count() > 1]


def row_order(size):
    far = diagonals(size)
    near = [1 << place for place in range(1, size.bit_length() - 1)]
    return far + near + [shift + 1 for shift in near] + [1]


def swap(block, shift, axis):
    size = lax.axis_size(axis)
    return lax.ppermute(block, axis, [(i, i ^ shift) for i in range(size)]) if shift else block


def shards(confidence, item_blocks, counts, item_factors):
    slots, width, _ = confidence.shape
    factor_width = item_factors.shape[1]
    groups = lax.axis_size("row")
    per_owner = slots // groups
    vmem = pl.BlockSpec(memory_space=pltpu.VMEM)
    smem = pl.BlockSpec(memory_space=pltpu.SMEM)

    params = pltpu.CompilerParams(vmem_limit_bytes=VMEM_LIMIT)

    def tiles(count):
        return jax.ShapeDtypeStruct((count, width, factor_width), item_factors.dtype)

    early = diagonals(groups)
    small = [jax.ShapeDtypeStruct(array.shape, array.dtype) for array in (item_blocks, counts, item_factors)]
    *loaded, blocks_here, counts_here, block_here = pl.pallas_call(
        load_kernel,
        out_shape=[tiles(per_owner if shift in early else 2 * per_owner) for shift in range(groups)] + small,
        in_specs=[pl.BlockSpec(memory_space=pl.ANY)] * 4,
        out_specs=[vmem] * (groups + 3),
        scratch_shapes=[pltpu.SemaphoreType.DMA((groups + 3,))],
        compiler_params=params,
    )(*[pltpu.with_memory_space_constraint(array, pltpu.HBM) for array in (confidence, item_blocks, counts, item_factors)])
    cols = lax.axis_size("col")
    blocks = [swap(item_factors, shift, "col") if shift else block_here for shift in col_order(cols)]
    weights = {shift: swap(loaded[shift], shift, "row") for shift in early}
    late = [shift for shift in range(groups) if shift not in early]
    parcels = pl.pallas_call(
        functools.partial(pick_kernel, groups, cols),
        out_shape=[tiles(per_owner if shift in early else 2 * per_owner) for shift in range(groups)],
        in_specs=[smem] * 2 + [vmem] * (cols + len(late)),
        out_specs=[vmem] * groups,
        input_output_aliases={2 + cols + place: shift for place, shift in enumerate(late)},
        scratch_shapes=[pltpu.VMEM((cols, width, factor_width), item_factors.dtype)],
        compiler_params=params,
    )(blocks_here, counts_here, *blocks, *[loaded[shift] for shift in late])
    items = {shift: swap(parcels[shift], shift, "row") for shift in [*row_order(groups), 0]}

    field = jax.ShapeDtypeStruct((width, factor_width), jnp.float32)
    b, q, v, u, stats = pl.pallas_call(
        krylov_kernel,
        out_shape=[field] * 4 + [jax.ShapeDtypeStruct((1, 1, factor_width), jnp.float32)],
        in_specs=[[vmem] * len(late), [[vmem] * 2] * len(early)],
        out_specs=[vmem] * 5,
        compiler_params=params,
    )([items[shift] for shift in items if shift in late], [[weights[shift], items[shift]] for shift in early])
    every = everyone(stats, ("row", "col"))
    return pl.pallas_call(
        finish_kernel,
        out_shape=[field] * 2,
        in_specs=[vmem] * 6,
        out_specs=[vmem] * 2,
        compiler_params=params,
    )(every, stats, b, q, v, u)


def solution(mesh):
    return jax.shard_map(
        shards,
        mesh=mesh,
        in_specs=(
            P(("row", "col"), None, None),
            P(("row", "col")),
            P(("row", "col")),
            P(("row", "col"), None),
        ),
        out_specs=(P(("row", "col"), None), P(("row", "col"), None)),
        check_vma=False,
    )
```

```python
import functools

import jax
import jax.numpy as jnp
from jax import lax
from jax.experimental import pallas as pl
from jax.experimental.pallas import tpu as pltpu
from jax.sharding import PartitionSpec as P

ridge = 2.0
PICK_FLOPS = 20_000_000_000
VMEM_LIMIT = 48 * 1024 * 1024
BB, BQ, VV, VB, VU, CROSS, STEP = range(7)


def dot(a, b, contract):
    return lax.dot_general(a, b, ((contract[:1], contract[1:]), ((), ())), preferred_element_type=jnp.float32)


def total(a):
    return jnp.sum(a, axis=(0, 1), keepdims=True)


def load_kernel(groups, confidence, item_blocks, counts, block, far, *refs):
    parcels, (marks, block_here, blocks_here, counts_here, arrived) = refs[:-5], refs[-5:]
    per_owner = confidence.shape[0] // groups
    cols = marks.shape[1]
    row, col = lax.axis_index("row"), lax.axis_index("col")
    pairs = [(item_blocks, blocks_here), (counts, counts_here)]
    targets = [(groups - 2, far, 0), (groups - 1, far, per_owner)]
    targets += [(shift, parcel, 0) for shift, parcel in enumerate(parcels)]
    pairs += [
        (confidence.at[pl.ds((row ^ shift) * per_owner, per_owner)], target.at[pl.ds(first, per_owner)])
        for shift, target, first in targets
    ]
    pairs.append((block, block_here))
    copies = [pltpu.make_async_copy(source, target, arrived.at[i]) for i, (source, target) in enumerate(pairs)]
    for copy in copies:
        copy.start()
    for copy in copies[:2]:
        copy.wait()
    shift_col = lax.broadcasted_iota(jnp.int32, marks.shape[1:], 0)
    for shift in range(groups):
        owner = row ^ shift
        for place in range(per_owner):
            chosen = jnp.where(place < counts_here[owner], blocks_here[owner * per_owner + place] ^ col, cols)

            marks[shift * per_owner + place] = jnp.where(shift_col == chosen, 1.0, 0.0).astype(marks.dtype)
    for copy in copies[2:]:
        copy.wait()


def pick_kernel(groups, cols, late, marks, *refs):
    blocks, (far, sibling, *parcels, slab) = refs[:cols], refs[cols + len(late):]
    for shift, block in zip(col_order(cols), blocks):
        slab[shift] = block[...]
    per_owner = marks.shape[0] // groups
    rows = marks.shape[2]
    targets = [(groups - 2, far, 0), (groups - 1, far, per_owner), (1, sibling, 0)]
    targets += [(shift, parcel, per_owner) for shift, parcel in zip(late, parcels)]
    for shift, target, first in targets:
        for place in range(per_owner):

            def add(shift_col, tile, slot=shift * per_owner + place):
                return tile + slab[shift_col].reshape(-1, *marks.shape[2:]) * marks[slot, shift_col][None]

            tile = jnp.zeros((slab.shape[1] // rows, *marks.shape[2:]), slab.dtype)
            tile = lax.fori_loop(0, cols, add, tile, unroll=cols <= 4)
            target[first + place] = tile.reshape(slab.shape[1:])


def tiles_of(far, sibling, whole):
    for weights, items in (far, sibling):
        part = weights.shape[0] // 2
        yield joined(weights[:part], items[:part])
    yield joined(sibling[0][part:], sibling[1][part:])
    for parcel in whole:
        yield joined(parcel[:part], parcel[part:])


def joined(weights, items):
    w = jnp.concatenate([weights[place] for place in range(weights.shape[0])], axis=1)
    return items.reshape(-1, items.shape[-1]), w


def apply(parts, field):
    low = field.astype(jnp.bfloat16)
    image = ridge * field
    energy = 0.0
    for x, w in tiles_of(*parts):
        scores = dot(low, x, (1, 1))
        weighted = w.astype(jnp.float32) * scores
        energy = energy + weighted * scores
        image = image + dot(weighted.astype(jnp.bfloat16), x, (1, 0))
    squares = total(field * field)
    return image, squares, ridge * squares + total(energy)


def krylov_kernel(far_items, whole, far_weights, sibling, b_ref, q_ref, v_ref, u_ref, stats):
    parts = (far_weights, far_items), sibling, whole
    b = jnp.zeros(b_ref.shape, jnp.float32)
    for x, w in tiles_of(*parts):
        b = b + dot(w, x, (1, 0))
    q, bb, bq = apply(parts, b)
    step = jnp.where(bq > 0, bb / bq, 1.0)
    v = b - step * q
    u, vv, vu = apply(parts, v)
    b_ref[...] = b
    q_ref[...] = q
    v_ref[...] = v
    u_ref[...] = u
    values = {BB: bb, BQ: bq, VV: vv, VB: total(v * b), VU: vu, CROSS: 2.0 * total(v * q), STEP: step}
    lane = lax.broadcasted_iota(jnp.int32, stats.shape[1:], 1)
    packed = jnp.zeros(stats.shape[1:], jnp.float32)
    for place, value in values.items():
        packed = jnp.where(lane == place, value, packed)
    stats[0] = packed


def finish_kernel(every, own, b_ref, q_ref, v_ref, u_ref, solution_ref, residual_ref):
    def field(place):
        return every[:, 0, place:place + 1]

    norm_now = jnp.sum(field(BB), axis=0, keepdims=True)
    step_0 = norm_now / jnp.sum(field(BQ), axis=0, keepdims=True)
    c1 = step_0 / field(STEP)
    rest = 1.0 - c1
    norm_next = jnp.sum(
        c1 * c1 * field(VV) + 2.0 * c1 * rest * field(VB) + rest * rest * field(BB), axis=0, keepdims=True
    )
    turn = norm_next / norm_now
    c2 = rest + turn
    bend = jnp.sum(c1 * c1 * field(VU) + c1 * c2 * field(CROSS) + c2 * c2 * field(BQ), axis=0, keepdims=True)
    step_1 = norm_next / bend
    c1 = step_0 / own[0, :, STEP:STEP + 1]
    rest = 1.0 - c1
    c2 = rest + turn
    b, v = b_ref[...], v_ref[...]
    solution_ref[...] = step_0 * b + step_1 * (c1 * v + c2 * b)
    residual_ref[...] = c1 * v + rest * b - step_1 * (c1 * u_ref[...] + c2 * q_ref[...])


def everyone(block, axes):
    size = lax.axis_size(axes)
    copies = jnp.broadcast_to(block[None], (size, *block.shape))
    return lax.all_to_all(copies, axes, split_axis=0, concat_axis=0, tiled=True).reshape(-1, *block.shape[1:])


def col_order(size):
    return [0, *sorted(range(1, size), key=lambda shift: shift != size >> 1)]


def row_order(size):
    near = [1 << place for place in range(1, size.bit_length() - 1)]
    near += [shift + 1 for shift in near]
    return [shift for shift in range(2, size - 2) if shift not in near] + near


def swap(block, shift, axis):
    size = lax.axis_size(axis)
    return lax.ppermute(block, axis, [(i, i ^ shift) for i in range(size)]) if shift else block


def shards(confidence, item_blocks, counts, item_factors):
    slots, width, _ = confidence.shape
    factor_width = item_factors.shape[1]
    groups = lax.axis_size("row")
    per_owner = slots // groups
    vmem = pl.BlockSpec(memory_space=pltpu.VMEM)

    params = pltpu.CompilerParams(vmem_limit_bytes=VMEM_LIMIT)

    def tiles(count):
        return jax.ShapeDtypeStruct((count, width, factor_width), item_factors.dtype)

    far = groups - 2
    cols = lax.axis_size("col")
    early, *loaded, marks, block_here = pl.pallas_call(
        functools.partial(load_kernel, groups),
        out_shape=[tiles(2 * per_owner if shift != 1 else per_owner) for shift in [far, *range(far)]]
        + [
            jax.ShapeDtypeStruct((slots, cols, 16, factor_width), item_factors.dtype),
            jax.ShapeDtypeStruct(item_factors.shape, item_factors.dtype),
        ],
        in_specs=[pl.BlockSpec(memory_space=pl.ANY)] * 4,
        out_specs=[vmem] * (far + 3),
        scratch_shapes=[
            pltpu.SMEM(item_blocks.shape, item_blocks.dtype),
            pltpu.SMEM(counts.shape, counts.dtype),
            pltpu.SemaphoreType.DMA((groups + 3,)),
        ],
        compiler_params=params,
    )(*[pltpu.with_memory_space_constraint(array, pltpu.HBM) for array in (confidence, item_blocks, counts, item_factors)])
    blocks = [swap(item_factors, shift, "col") if shift else block_here for shift in col_order(cols)]
    early = swap(early, far, "row")
    late = [0, *row_order(groups)]
    far_items, sibling_items, *parcels = pl.pallas_call(
        functools.partial(pick_kernel, groups, cols, late),
        out_shape=[tiles(2 * per_owner), tiles(per_owner)] + [tiles(2 * per_owner)] * len(late),
        in_specs=[vmem] * (1 + cols + len(late)),
        out_specs=[vmem] * (2 + len(late)),
        input_output_aliases={1 + cols + place: 2 + place for place in range(len(late))},
        scratch_shapes=[pltpu.VMEM((cols, width, factor_width), item_factors.dtype)],
        cost_estimate=pl.CostEstimate(flops=PICK_FLOPS, bytes_accessed=0, transcendentals=0),
        compiler_params=params,
    )(marks, *blocks, *[loaded[shift] for shift in late])
    far_items = swap(far_items, far, "row")
    whole = [swap(parcel, shift, "row") for shift, parcel in zip(late, parcels)]
    sibling = [
        swap(jnp.concatenate([own, passed[per_owner:]]), 1, "row")
        for own, passed in ((loaded[1], early), (sibling_items, far_items))
    ]

    field = jax.ShapeDtypeStruct((width, factor_width), jnp.float32)
    b, q, v, u, stats = pl.pallas_call(
        krylov_kernel,
        out_shape=[field] * 4 + [jax.ShapeDtypeStruct((1, 1, factor_width), jnp.float32)],
        in_specs=[vmem, [vmem] * len(whole), vmem, [vmem] * 2],
        out_specs=[vmem] * 5,
        compiler_params=params,
    )(far_items, whole, early, sibling)
    every = everyone(stats, ("row", "col"))
    return pl.pallas_call(
        finish_kernel,
        out_shape=[field] * 2,
        in_specs=[vmem] * 6,
        out_specs=[vmem] * 2,
        compiler_params=params,
    )(every, stats, b, q, v, u)


def solution(mesh):
    return jax.shard_map(
        shards,
        mesh=mesh,
        in_specs=(
            P(("row", "col"), None, None),
            P(("row", "col")),
            P(("row", "col")),
            P(("row", "col"), None),
        ),
        out_specs=(P(("row", "col"), None), P(("row", "col"), None)),
        check_vma=False,
    )
```

```python
import functools

import jax
import jax.numpy as jnp
from jax import lax
from jax.experimental import pallas as pl
from jax.experimental.pallas import tpu as pltpu
from jax.sharding import PartitionSpec as P

ridge = 2.0
PICK_FLOPS = 20_000_000_000
VMEM_LIMIT = 48 * 1024 * 1024
BB, BQ, VV, VB, VU, CROSS, STEP = range(7)


def dot(a, b, contract):
    return lax.dot_general(a, b, ((contract[:1], contract[1:]), ((), ())), preferred_element_type=jnp.float32)


def total(a):
    return jnp.sum(a, axis=(0, 1), keepdims=True)


def load_kernel(groups, confidence, item_blocks, counts, block, far, *refs):
    parcels, (marks, block_here, blocks_here, counts_here, arrived) = refs[:-5], refs[-5:]
    per_owner = confidence.shape[0] // groups
    cols = marks.shape[1]
    row, col = lax.axis_index("row"), lax.axis_index("col")
    pairs = [(item_blocks, blocks_here), (counts, counts_here)]
    targets = [(groups - 2, far, 0), (groups - 1, far, per_owner)]
    targets += [(shift, parcel, 0) for shift, parcel in enumerate(parcels)]
    pairs += [
        (confidence.at[pl.ds((row ^ shift) * per_owner, per_owner)], target.at[pl.ds(first, per_owner)])
        for shift, target, first in targets
    ]
    pairs.append((block, block_here))
    copies = [pltpu.make_async_copy(source, target, arrived.at[i]) for i, (source, target) in enumerate(pairs)]
    for copy in copies:
        copy.start()
    for copy in copies[:2]:
        copy.wait()
    shift_col = lax.broadcasted_iota(jnp.int32, marks.shape[1:], 0)
    for shift in range(groups):
        owner = row ^ shift
        for place in range(per_owner):
            chosen = jnp.where(place < counts_here[owner], blocks_here[owner * per_owner + place] ^ col, cols)

            marks[shift * per_owner + place] = jnp.where(shift_col == chosen, 1.0, 0.0).astype(marks.dtype)
    for copy in copies[2:]:
        copy.wait()


def pick_kernel(groups, cols, late, marks, *refs):
    blocks, (far, sibling, *parcels, slab) = refs[:cols], refs[cols + len(late):]
    for shift, block in zip(col_order(cols), blocks):
        slab[shift] = block[...]
    per_owner = marks.shape[0] // groups
    rows = marks.shape[2]
    targets = [(groups - 2, far, 0), (groups - 1, far, per_owner), (1, sibling, 0)]
    targets += [(shift, parcel, per_owner) for shift, parcel in zip(late, parcels)]
    for shift, target, first in targets:
        for place in range(per_owner):

            def add(shift_col, tile, slot=shift * per_owner + place):
                return tile + slab[shift_col].reshape(-1, *marks.shape[2:]) * marks[slot, shift_col][None]

            tile = jnp.zeros((slab.shape[1] // rows, *marks.shape[2:]), slab.dtype)
            tile = lax.fori_loop(0, cols, add, tile, unroll=cols <= 4)
            target[first + place] = tile.reshape(slab.shape[1:])


def tiles_of(far, sibling, whole):
    for weights, items in (far, sibling):
        part = weights.shape[0] // 2
        yield joined(weights[:part], items[:part])
    yield joined(sibling[0][part:], sibling[1][part:])
    for parcel in whole:
        yield joined(parcel[:part], parcel[part:])


def joined(weights, items):
    w = jnp.concatenate([weights[place] for place in range(weights.shape[0])], axis=1)
    return items.reshape(-1, items.shape[-1]), w


def apply(parts, field):
    low = field.astype(jnp.bfloat16)
    image = ridge * field
    energy = 0.0
    for x, w in tiles_of(*parts):
        scores = dot(low, x, (1, 1))
        weighted = w.astype(jnp.float32) * scores
        energy = energy + weighted * scores
        image = image + dot(weighted.astype(jnp.bfloat16), x, (1, 0))
    squares = total(field * field)
    return image, squares, ridge * squares + total(energy)


def krylov_kernel(far_items, whole, far_weights, sibling, b_ref, q_ref, v_ref, u_ref, stats):
    parts = (far_weights, far_items), sibling, whole
    b = jnp.zeros(b_ref.shape, jnp.float32)
    for x, w in tiles_of(*parts):
        b = b + dot(w, x, (1, 0))
    q, bb, bq = apply(parts, b)
    step = jnp.where(bq > 0, bb / bq, 1.0)
    v = b - step * q
    u, vv, vu = apply(parts, v)
    b_ref[...] = b
    q_ref[...] = q
    v_ref[...] = v
    u_ref[...] = u
    values = {BB: bb, BQ: bq, VV: vv, VB: total(v * b), VU: vu, CROSS: 2.0 * total(v * q), STEP: step}
    lane = lax.broadcasted_iota(jnp.int32, stats.shape[1:], 1)
    packed = jnp.zeros(stats.shape[1:], jnp.float32)
    for place, value in values.items():
        packed = jnp.where(lane == place, value, packed)
    stats[0] = packed


def finish_kernel(every, own, b_ref, q_ref, v_ref, u_ref, solution_ref, residual_ref):
    def field(place):
        return every[:, 0, place:place + 1]

    norm_now = jnp.sum(field(BB), axis=0, keepdims=True)
    step_0 = norm_now / jnp.sum(field(BQ), axis=0, keepdims=True)
    c1 = step_0 / field(STEP)
    rest = 1.0 - c1
    norm_next = jnp.sum(
        c1 * c1 * field(VV) + 2.0 * c1 * rest * field(VB) + rest * rest * field(BB), axis=0, keepdims=True
    )
    turn = norm_next / norm_now
    c2 = rest + turn
    bend = jnp.sum(c1 * c1 * field(VU) + c1 * c2 * field(CROSS) + c2 * c2 * field(BQ), axis=0, keepdims=True)
    step_1 = norm_next / bend
    c1 = step_0 / own[0, :, STEP:STEP + 1]
    rest = 1.0 - c1
    c2 = rest + turn
    b, v = b_ref[...], v_ref[...]
    solution_ref[...] = step_0 * b + step_1 * (c1 * v + c2 * b)
    residual_ref[...] = c1 * v + rest * b - step_1 * (c1 * u_ref[...] + c2 * q_ref[...])


def everyone(block, axes):
    size = lax.axis_size(axes)
    copies = jnp.broadcast_to(block[None], (size, *block.shape))
    return lax.all_to_all(copies, axes, split_axis=0, concat_axis=0, tiled=True).reshape(-1, *block.shape[1:])


def col_order(size):
    return [0, *sorted(range(1, size), key=lambda shift: shift != size >> 1)]


def row_order(size):
    near = [1 << place for place in range(1, size.bit_length() - 1)]
    near += [shift + 1 for shift in near[::-1]]
    return [shift for shift in range(2, size - 2) if shift not in near] + near


def swap(block, shift, axis):
    size = lax.axis_size(axis)
    return lax.ppermute(block, axis, [(i, i ^ shift) for i in range(size)]) if shift else block


def shards(confidence, item_blocks, counts, item_factors):
    slots, width, _ = confidence.shape
    factor_width = item_factors.shape[1]
    groups = lax.axis_size("row")
    per_owner = slots // groups
    vmem = pl.BlockSpec(memory_space=pltpu.VMEM)

    params = pltpu.CompilerParams(vmem_limit_bytes=VMEM_LIMIT)

    def tiles(count):
        return jax.ShapeDtypeStruct((count, width, factor_width), item_factors.dtype)

    far = groups - 2
    cols = lax.axis_size("col")
    early, *loaded, marks, block_here = pl.pallas_call(
        functools.partial(load_kernel, groups),
        out_shape=[tiles(2 * per_owner if shift != 1 else per_owner) for shift in [far, *range(far)]]
        + [
            jax.ShapeDtypeStruct((slots, cols, 16, factor_width), item_factors.dtype),
            jax.ShapeDtypeStruct(item_factors.shape, item_factors.dtype),
        ],
        in_specs=[pl.BlockSpec(memory_space=pl.ANY)] * 4,
        out_specs=[vmem] * (far + 3),
        scratch_shapes=[
            pltpu.SMEM(item_blocks.shape, item_blocks.dtype),
            pltpu.SMEM(counts.shape, counts.dtype),
            pltpu.SemaphoreType.DMA((groups + 3,)),
        ],
        compiler_params=params,
    )(*[pltpu.with_memory_space_constraint(array, pltpu.HBM) for array in (confidence, item_blocks, counts, item_factors)])
    blocks = [swap(item_factors, shift, "col") if shift else block_here for shift in col_order(cols)]
    early = swap(early, far, "row")
    late = [0, *row_order(groups)]
    far_items, sibling_items, *parcels = pl.pallas_call(
        functools.partial(pick_kernel, groups, cols, late),
        out_shape=[tiles(2 * per_owner), tiles(per_owner)] + [tiles(2 * per_owner)] * len(late),
        in_specs=[vmem] * (1 + cols + len(late)),
        out_specs=[vmem] * (2 + len(late)),
        input_output_aliases={1 + cols + place: 2 + place for place in range(len(late))},
        scratch_shapes=[pltpu.VMEM((cols, width, factor_width), item_factors.dtype)],
        cost_estimate=pl.CostEstimate(flops=PICK_FLOPS, bytes_accessed=0, transcendentals=0),
        compiler_params=params,
    )(marks, *blocks, *[loaded[shift] for shift in late])
    far_items = swap(far_items, far, "row")
    whole = [swap(parcel, shift, "row") for shift, parcel in zip(late, parcels)]
    sibling = [
        swap(jnp.concatenate([own, passed[per_owner:]]), 1, "row")
        for own, passed in ((loaded[1], early), (sibling_items, far_items))
    ]

    field = jax.ShapeDtypeStruct((width, factor_width), jnp.float32)
    b, q, v, u, stats = pl.pallas_call(
        krylov_kernel,
        out_shape=[field] * 4 + [jax.ShapeDtypeStruct((1, 1, factor_width), jnp.float32)],
        in_specs=[vmem, [vmem] * len(whole), vmem, [vmem] * 2],
        out_specs=[vmem] * 5,
        compiler_params=params,
    )(far_items, whole, early, sibling)
    every = everyone(stats, ("row", "col"))
    return pl.pallas_call(
        finish_kernel,
        out_shape=[field] * 2,
        in_specs=[vmem] * 6,
        out_specs=[vmem] * 2,
        compiler_params=params,
    )(every, stats, b, q, v, u)


def solution(mesh):
    return jax.shard_map(
        shards,
        mesh=mesh,
        in_specs=(
            P(("row", "col"), None, None),
            P(("row", "col")),
            P(("row", "col")),
            P(("row", "col"), None),
        ),
        out_specs=(P(("row", "col"), None), P(("row", "col"), None)),
        check_vma=False,
    )
```

```python
import functools

import jax
import jax.numpy as jnp
from jax import lax
from jax.experimental import pallas as pl
from jax.experimental.pallas import tpu as pltpu
from jax.sharding import PartitionSpec as P

ridge = 2.0
PICK_FLOPS = 20_000_000_000
VMEM_LIMIT = 48 * 1024 * 1024
BB, BQ, VV, VB, VU, CROSS, STEP = range(7)


def dot(a, b, contract):
    return lax.dot_general(a, b, ((contract[:1], contract[1:]), ((), ())), preferred_element_type=jnp.float32)


def total(a):
    return jnp.sum(a, axis=(0, 1), keepdims=True)


def load_kernel(groups, confidence, item_blocks, counts, block, far, *refs):
    parcels, (marks, block_here, blocks_here, counts_here, arrived) = refs[:-5], refs[-5:]
    per_owner = confidence.shape[0] // groups
    cols = marks.shape[1]
    row, col = lax.axis_index("row"), lax.axis_index("col")
    pairs = [(item_blocks, blocks_here), (counts, counts_here)]
    targets = [(groups - 1, far, 0), (groups - 2, far, per_owner)]
    targets += [(shift, parcel, 0) for shift, parcel in enumerate(parcels)]
    pairs += [
        (confidence.at[pl.ds((row ^ shift) * per_owner, per_owner)], target.at[pl.ds(first, per_owner)])
        for shift, target, first in targets
    ]
    pairs.append((block, block_here))
    copies = [pltpu.make_async_copy(source, target, arrived.at[i]) for i, (source, target) in enumerate(pairs)]
    for copy in copies:
        copy.start()
    for copy in copies[:2]:
        copy.wait()
    shift_col = lax.broadcasted_iota(jnp.int32, marks.shape[1:], 0)
    for shift in range(groups):
        owner = row ^ shift
        for place in range(per_owner):
            chosen = jnp.where(place < counts_here[owner], blocks_here[owner * per_owner + place] ^ col, cols)

            marks[shift * per_owner + place] = jnp.where(shift_col == chosen, 1.0, 0.0).astype(marks.dtype)
    for copy in copies[2:]:
        copy.wait()


def pick_kernel(groups, cols, late, marks, *refs):
    blocks, (far, sibling, *parcels, slab) = refs[:cols], refs[cols + len(late):]
    for shift, block in zip(col_order(cols), blocks):
        slab[shift] = block[...]
    per_owner = marks.shape[0] // groups
    rows = marks.shape[2]
    targets = [(groups - 1, far, 0), (groups - 2, far, per_owner), (1, sibling, 0)]
    targets += [(shift, parcel, per_owner) for shift, parcel in zip(late, parcels)]
    for shift, target, first in targets:
        for place in range(per_owner):

            def add(shift_col, tile, slot=shift * per_owner + place):
                return tile + slab[shift_col].reshape(-1, *marks.shape[2:]) * marks[slot, shift_col][None]

            tile = jnp.zeros((slab.shape[1] // rows, *marks.shape[2:]), slab.dtype)
            tile = lax.fori_loop(0, cols, add, tile, unroll=cols <= 4)
            target[first + place] = tile.reshape(slab.shape[1:])


def tiles_of(far, sibling, whole):
    for weights, items in (far, sibling):
        part = weights.shape[0] // 2
        yield joined(weights[:part], items[:part])
    yield joined(sibling[0][part:], sibling[1][part:])
    for parcel in whole:
        yield joined(parcel[:part], parcel[part:])


def joined(weights, items):
    w = jnp.concatenate([weights[place] for place in range(weights.shape[0])], axis=1)
    return items.reshape(-1, items.shape[-1]), w


def apply(parts, field):
    low = field.astype(jnp.bfloat16)
    image = ridge * field
    energy = 0.0
    for x, w in tiles_of(*parts):
        scores = dot(low, x, (1, 1))
        weighted = w.astype(jnp.float32) * scores
        energy = energy + weighted * scores
        image = image + dot(weighted.astype(jnp.bfloat16), x, (1, 0))
    squares = total(field * field)
    return image, squares, ridge * squares + total(energy)


def krylov_kernel(far_items, whole, far_weights, sibling, b_ref, q_ref, v_ref, u_ref, stats):
    parts = (far_weights, far_items), sibling, whole
    b = jnp.zeros(b_ref.shape, jnp.float32)
    for x, w in tiles_of(*parts):
        b = b + dot(w, x, (1, 0))
    q, bb, bq = apply(parts, b)
    step = jnp.where(bq > 0, bb / bq, 1.0)
    v = b - step * q
    u, vv, vu = apply(parts, v)
    b_ref[...] = b
    q_ref[...] = q
    v_ref[...] = v
    u_ref[...] = u
    values = {BB: bb, BQ: bq, VV: vv, VB: total(v * b), VU: vu, CROSS: 2.0 * total(v * q), STEP: step}
    lane = lax.broadcasted_iota(jnp.int32, stats.shape[1:], 1)
    packed = jnp.zeros(stats.shape[1:], jnp.float32)
    for place, value in values.items():
        packed = jnp.where(lane == place, value, packed)
    stats[0] = packed


def finish_kernel(every, own, b_ref, q_ref, v_ref, u_ref, solution_ref, residual_ref):
    def field(place):
        return every[:, 0, place:place + 1]

    norm_now = jnp.sum(field(BB), axis=0, keepdims=True)
    step_0 = norm_now / jnp.sum(field(BQ), axis=0, keepdims=True)
    c1 = step_0 / field(STEP)
    rest = 1.0 - c1
    norm_next = jnp.sum(
        c1 * c1 * field(VV) + 2.0 * c1 * rest * field(VB) + rest * rest * field(BB), axis=0, keepdims=True
    )
    turn = norm_next / norm_now
    c2 = rest + turn
    bend = jnp.sum(c1 * c1 * field(VU) + c1 * c2 * field(CROSS) + c2 * c2 * field(BQ), axis=0, keepdims=True)
    step_1 = norm_next / bend
    c1 = step_0 / own[0, :, STEP:STEP + 1]
    rest = 1.0 - c1
    c2 = rest + turn
    b, v = b_ref[...], v_ref[...]
    solution_ref[...] = step_0 * b + step_1 * (c1 * v + c2 * b)
    residual_ref[...] = c1 * v + rest * b - step_1 * (c1 * u_ref[...] + c2 * q_ref[...])


def everyone(block, axes):
    size = lax.axis_size(axes)
    copies = jnp.broadcast_to(block[None], (size, *block.shape))
    return lax.all_to_all(copies, axes, split_axis=0, concat_axis=0, tiled=True).reshape(-1, *block.shape[1:])


def col_order(size):
    return [0, *sorted(range(1, size), key=lambda shift: shift != size >> 1)]


def row_order(size):
    near = [1 << place for place in range(1, size.bit_length() - 1)]
    near += [shift + 1 for shift in near[::-1]]
    return [shift for shift in range(2, size - 2) if shift not in near] + near


def swap(block, shift, axis):
    size = lax.axis_size(axis)
    return lax.ppermute(block, axis, [(i, i ^ shift) for i in range(size)]) if shift else block


def shards(confidence, item_blocks, counts, item_factors):
    slots, width, _ = confidence.shape
    factor_width = item_factors.shape[1]
    groups = lax.axis_size("row")
    per_owner = slots // groups
    vmem = pl.BlockSpec(memory_space=pltpu.VMEM)

    params = pltpu.CompilerParams(vmem_limit_bytes=VMEM_LIMIT)

    def tiles(count):
        return jax.ShapeDtypeStruct((count, width, factor_width), item_factors.dtype)

    far = groups - 1
    cols = lax.axis_size("col")
    early, *loaded, marks, block_here = pl.pallas_call(
        functools.partial(load_kernel, groups),
        out_shape=[tiles(2 * per_owner if shift != 1 else per_owner) for shift in [far, *range(groups - 2)]]
        + [
            jax.ShapeDtypeStruct((slots, cols, 16, factor_width), item_factors.dtype),
            jax.ShapeDtypeStruct(item_factors.shape, item_factors.dtype),
        ],
        in_specs=[pl.BlockSpec(memory_space=pl.ANY)] * 4,
        out_specs=[vmem] * (groups + 1),
        scratch_shapes=[
            pltpu.SMEM(item_blocks.shape, item_blocks.dtype),
            pltpu.SMEM(counts.shape, counts.dtype),
            pltpu.SemaphoreType.DMA((groups + 3,)),
        ],
        compiler_params=params,
    )(*[pltpu.with_memory_space_constraint(array, pltpu.HBM) for array in (confidence, item_blocks, counts, item_factors)])
    blocks = [swap(item_factors, shift, "col") if shift else block_here for shift in col_order(cols)]
    early = swap(early, far, "row")
    late = [0, *row_order(groups)]
    far_items, sibling_items, *parcels = pl.pallas_call(
        functools.partial(pick_kernel, groups, cols, late),
        out_shape=[tiles(2 * per_owner), tiles(per_owner)] + [tiles(2 * per_owner)] * len(late),
        in_specs=[vmem] * (1 + cols + len(late)),
        out_specs=[vmem] * (2 + len(late)),
        input_output_aliases={1 + cols + place: 2 + place for place in range(len(late))},
        scratch_shapes=[pltpu.VMEM((cols, width, factor_width), item_factors.dtype)],
        cost_estimate=pl.CostEstimate(flops=PICK_FLOPS, bytes_accessed=0, transcendentals=0),
        compiler_params=params,
    )(marks, *blocks, *[loaded[shift] for shift in late])
    far_items = swap(far_items, far, "row")
    whole = [swap(parcel, shift, "row") for shift, parcel in zip(late, parcels)]
    sibling = [
        swap(jnp.concatenate([own, passed[per_owner:]]), 1, "row")
        for own, passed in ((loaded[1], early), (sibling_items, far_items))
    ]

    field = jax.ShapeDtypeStruct((width, factor_width), jnp.float32)
    b, q, v, u, stats = pl.pallas_call(
        krylov_kernel,
        out_shape=[field] * 4 + [jax.ShapeDtypeStruct((1, 1, factor_width), jnp.float32)],
        in_specs=[vmem, [vmem] * len(whole), vmem, [vmem] * 2],
        out_specs=[vmem] * 5,
        compiler_params=params,
    )(far_items, whole, early, sibling)
    every = everyone(stats, ("row", "col"))
    return pl.pallas_call(
        finish_kernel,
        out_shape=[field] * 2,
        in_specs=[vmem] * 6,
        out_specs=[vmem] * 2,
        compiler_params=params,
    )(every, stats, b, q, v, u)


def solution(mesh):
    return jax.shard_map(
        shards,
        mesh=mesh,
        in_specs=(
            P(("row", "col"), None, None),
            P(("row", "col")),
            P(("row", "col")),
            P(("row", "col"), None),
        ),
        out_specs=(P(("row", "col"), None), P(("row", "col"), None)),
        check_vma=False,
    )
```
